32 devices in a mesh: view: 2 (over y), slab: 16 (over z, x, core).
Axes of the slice: x: 2, y: 2, z: 4, core: 2. Of those that a mesh axis runs over, the one named last changes fastest.
Arguments:
- estimate: float32 [16, 256, 1024], P('slab'), may hold values from 0.5 to 2
- measured: float32 [2, 16, 256, 1024], P('view', None, 'slab'), may hold values from 0.5 to 2
- offsets: int32 [2], P('view'), may hold values from 0 to 15, as said below
- mirrors: int32 [2, 2], P('view'), may hold values from 0 to 1
- psf: float32 [2, 3, 17], P('view'), may hold values from 0.002 to 1, as said below
Outputs:
- updated: float32 [16, 256, 1024], P('slab')
The draws below stay inside these ranges and needn't reach their ends.
Inputs may be any that keep to these rules, and one draw needn't show every extreme that they name: `psf`: every tap is positive. The views' offsets are distinct, and one view has the last block offset.
All inputs are finite; a program needn't handle non-finite values.
Results may differ from the reference program's by a relative error of at most 0.0003.
Values sent between devices are 32-bit elements; how exact they have to be, the bound alone decides.
No kernel may reach another device: no remote copies, remote signals or barrier semaphores. Data moves between devices by JAX's collectives and lax.ppermute only.
A program may use at most 64 MiB of HBM per device.

```python
import math
import jax
import jax.numpy as jnp
from jax import lax

VIEWS = 2
TAPS = 17
BLOCK = 64
NX = 1024
NZ = 16
NY = 256


def draw_psf(key, part):
    key_side = jax.random.fold_in(key, 11)
    key_mid = jax.random.fold_in(key, 12)
    sidelobe = jnp.exp(jax.random.uniform(key_side, (VIEWS, 3, TAPS), jnp.float32, -6.0, -2.0))
    centre = 0.5 + 0.5 * jax.random.uniform(key_mid, (VIEWS, 3, 1), jnp.float32)
    middle = jnp.arange(TAPS) == TAPS // 2
    return jnp.where(middle[None, None, :], centre, sidelobe).astype(jnp.float32)


def draw_offsets(key, part):
    key_perm = jax.random.fold_in(key, 21)
    key_slot = jax.random.fold_in(key, 22)
    block_count = NX // BLOCK
    others = jax.random.permutation(key_perm, block_count - 1).astype(jnp.int32)[:VIEWS - 1]
    values = jnp.concatenate([jnp.full((1,), block_count - 1, jnp.int32), others])
    slot = jax.random.randint(key_slot, (), 0, VIEWS)
    return jnp.roll(values, slot).astype(jnp.int32)


def plant(result, rng, smallest, top_value):
    longest = result.shape.index(max(result.shape))
    spots = []
    for shift in (0, 1):
        where = [jax.random.randint(jax.random.fold_in(rng, axis), (), 0, length) for axis, length in enumerate(result.shape)]
        where[longest] = (where[longest] + shift) % result.shape[longest]
        spots.append(tuple(where))
    return result.at[spots[0]].set(smallest).at[spots[1]].set(top_value)


def shard_levels(key, extent, shards, low, largest):
    def one(axis_at, blocks):
        heights = jax.random.uniform(jax.random.fold_in(jax.random.fold_in(key, 6), axis_at), (blocks,), jnp.float32, low / len(shards), largest / len(shards))
        return jnp.repeat(jnp.exp(heights), extent[axis_at] // blocks).reshape((-1,) + (1,) * (len(extent) - axis_at - 1))

    factor_of = one(*shards[0])
    for cut in shards[1:]:
        factor_of = factor_of * one(*cut)
    return factor_of


def setup_inputs(seed: int = 0) -> dict:
    streams_of = jax.random.split(jax.random.key(seed), 6)
    return {
        "estimate": jnp.clip(jnp.exp(math.log(2.0) - 1.3862944 * jax.random.uniform(streams_of[0], (NZ, NY, NX), jnp.float32) ** shard_levels(streams_of[0], (NZ, NY, NX), ((0, 16),), -0.2, 0.2)), 0.5, 2.0),
        "measured": jnp.clip(jnp.exp(math.log(2.0) - 1.3862944 * jax.random.uniform(streams_of[1], (VIEWS, NZ, NY, NX), jnp.float32) ** shard_levels(streams_of[1], (VIEWS, NZ, NY, NX), ((0, 2), (2, 16)), -0.2, 0.2)), 0.5, 2.0),
        "offsets": draw_offsets(jax.random.fold_in(streams_of[5], 71), 0),
        "mirrors": plant(jax.random.randint(streams_of[3], (VIEWS, 2), 0, 2), jax.random.fold_in(streams_of[3], 1), 0, 1).astype(jnp.int32),
        "psf": draw_psf(jax.random.fold_in(streams_of[5], 71), 0),
    }


def convolve(volume, tap_row, axis_dim, reverse):
    tap_count = tap_row.shape[0]
    radius = tap_count // 2
    if reverse:
        tap_row = tap_row[::-1]
    widths = [(0, 0)] * volume.ndim
    widths[axis_dim] = (radius, radius)
    padded = jnp.pad(volume, widths)
    length = volume.shape[axis_dim]
    summed = tap_row[0] * lax.slice_in_dim(padded, 0, length, axis=axis_dim)
    for tap_index in range(1, tap_count):
        summed = summed + tap_row[tap_index] * lax.slice_in_dim(padded, tap_index, tap_index + length, axis=axis_dim)
    return summed


def resample(volume, shift_blocks, mirror_z, mirror_x):
    volume = lax.cond(mirror_z == 1, lambda arr: jnp.flip(arr, 0), lambda arr: arr, volume)
    volume = lax.cond(mirror_x == 1, lambda arr: jnp.flip(arr, 2), lambda arr: arr, volume)
    return jnp.roll(volume, shift_blocks * BLOCK, axis=2)


def unresample(volume, shift_blocks, mirror_z, mirror_x):
    volume = jnp.roll(volume, -shift_blocks * BLOCK, axis=2)
    volume = lax.cond(mirror_x == 1, lambda arr: jnp.flip(arr, 2), lambda arr: arr, volume)
    return lax.cond(mirror_z == 1, lambda arr: jnp.flip(arr, 0), lambda arr: arr, volume)


def reference(estimate, measured, offsets, mirrors, psf):
    factor = jnp.ones_like(estimate)
    for view_index in range(VIEWS):
        framed = resample(estimate, offsets[view_index], mirrors[view_index, 0], mirrors[view_index, 1])
        blurred = convolve(framed, psf[view_index, 0], 0, False)
        blurred = convolve(blurred, psf[view_index, 1], 1, False)
        blurred = convolve(blurred, psf[view_index, 2], 2, False)
        ratio = measured[view_index] / blurred
        spread = convolve(ratio, psf[view_index, 2], 2, True)
        spread = convolve(spread, psf[view_index, 1], 1, True)
        spread = convolve(spread, psf[view_index, 0], 0, True)
        factor = factor * unresample(spread, offsets[view_index], mirrors[view_index, 0], mirrors[view_index, 1])
    return estimate * factor
```

```python
import functools

import jax
import jax.numpy as jnp
from jax import lax
from jax.experimental import pallas as pl
from jax.experimental.pallas import tpu as pltpu
from jax.sharding import PartitionSpec as P

BLOCK = 64
TILE = 256
LANES = 128
CHUNKS = 2
LOW = 4
PACKED = 16
RATIO_BYTES = 12 * 1024 * 1024
OTHER_BYTES = 6 * 1024 * 1024
VMEM_BYTES = 48 * 1024 * 1024


def split(value):
    high = value.astype(jnp.bfloat16)
    low = (value - high.astype(jnp.float32)).astype(jnp.bfloat16)
    return high, low


def dot3(left, right):
    def dot(a, b):
        return jnp.dot(a, b, preferred_element_type=jnp.float32)

    return dot(left[0], right[0]) + (dot(left[0], right[1]) + dot(left[1], right[0]))


def toeplitz(taps, place):
    out = jnp.zeros(place.shape, jnp.float32)
    for index, tap in enumerate(taps):
        out = jnp.where(place == index, tap, out)
    return out


def y_cells(index, start, rows, chunks):
    step = rows // chunks
    count = index.shape[0] * index.shape[1] // chunks
    chunk = index // count
    within = index % count
    return start + (within // step) * rows + chunk * step + within % step


def y_band(taps, targets, sources):
    return split(toeplitz(taps, sources - targets + len(taps) // 2))


def y_window(first, height):
    window = min(2 * TILE, height)
    if height <= TILE:
        return 0, window
    return pl.multiple_of(jnp.clip(first - LANES, 0, height - window), LANES), window


def taps_of(psf_ref, row):
    return [psf_ref[0, row, t] for t in range(psf_ref.shape[2])]


def iota(shape, dimension):
    return lax.broadcasted_iota(jnp.int32, shape, dimension)


THERE = ("lh", "hl")
BACK = ("lh", "hl")


def order_of(plan, chunk, slabs):
    digits = {"l": (LOW, 1), "h": (slabs // LOW, LOW)}
    return tuple(digits[name] for name in plan[chunk])


def place_of(index, plan, chunk, slabs):
    return tuple(index // unit % radix for radix, unit in order_of(plan, chunk, slabs))


def first_message(plan, chunk, slabs, stage):
    return sum(order_of(plan, c, slabs)[stage][0] for c in range(chunk))


def blur_y_kernel(chunk, psf_ref, est_ref, *refs):
    out_refs = refs[-LOW:] if THERE[chunk] == "lh" else refs
    me = lax.axis_index("slab")
    height, width = est_ref.shape[1:]
    step = out_refs[0].shape[1]
    rows = step * CHUNKS
    slabs = height // rows
    lines = min(TILE, height) // CHUNKS
    blocks = lines // step
    taps = taps_of(psf_ref, 1)
    line = iota((lines, 1), 0)
    for group in range(slabs // blocks):
        targets = ((line // step + group * blocks) ^ me) * rows + chunk * step + line % step
        first = ((group * blocks) ^ (me // blocks * blocks)) * rows
        start, window = y_window(first, height)
        band = y_band(taps, targets, start + iota((1, window), 1))
        for x in range(0, width, TILE):
            value = dot3(band, split(est_ref[0, pl.ds(start, window), x : x + TILE]))
            for block in range(blocks):
                message, at = place_of(group * blocks + block, THERE, chunk, slabs)
                out_refs[message][at, :, x : x + TILE] = value[block * step : (block + 1) * step]


def x_position(cell, width, shift, flip):
    place = jnp.where(flip, width - 1 - cell, cell) + shift
    return jnp.where(place >= width, place - width, place)


def ratio_kernel(chunk, offset_ref, mirror_ref, psf_ref, meas_ref, *refs):
    work_ref, out_ref, high_ref, low_ref = refs[-4:]
    me = lax.axis_index("slab")
    depth, rows, width = work_ref.shape
    last = order_of(THERE, chunk, depth)[-1][0]
    arrived, leaving = refs[:last], refs[last:-4]
    for index in range(depth):
        at, message = place_of(index, THERE, chunk, depth)
        work_ref[me ^ index] = arrived[message][at]
    tap_count = psf_ref.shape[2]
    radius = tap_count // 2
    flip_z = mirror_ref[0, 0] == 1
    flip_x = mirror_ref[0, 1] == 1
    shift = offset_ref[0] * BLOCK

    def oriented(row, flip):
        taps = taps_of(psf_ref, row)
        return [jnp.where(flip, taps[tap_count - 1 - t], taps[t]) for t in range(tap_count)]

    z_taps = oriented(0, flip_z)
    x_taps = oriented(2, flip_x)

    def filter_z(load, store, taps):
        for z in range(depth):
            total = None
            for t in range(tap_count):
                source = z + t - radius
                if 0 <= source < depth:
                    term = taps[t] * load(source)
                    total = term if total is None else total + term
            store(z, total)

    group = max(1, PACKED // rows)

    @pl.loop(0, width // LANES)
    def _(index):
        lanes = pl.ds(pl.multiple_of(index * LANES, LANES), LANES)
        inner = pl.ds(pl.multiple_of((index + 1) * LANES, LANES), LANES)
        held = []

        def put(z, value):
            held.append(value)
            if len(held) == group:
                high, low = split(jnp.concatenate(held))
                where = pl.ds((z + 1 - group) * rows, group * rows)
                high_ref[where, inner] = high
                low_ref[where, inner] = low
                held.clear()

        filter_z(lambda z: work_ref[z, :, lanes], put, z_taps)

    def wrap():
        for ref in (high_ref, low_ref):
            ref[:, 0:LANES] = ref[:, width : width + LANES]
            ref[:, width + LANES : width + 2 * LANES] = ref[:, LANES : 2 * LANES]

    window = TILE + 2 * LANES
    shape = (window, TILE)
    place = (
        lax.broadcasted_iota(jnp.int32, shape, 0)
        - lax.broadcasted_iota(jnp.int32, shape, 1)
        + (radius - LANES)
    )
    bands = (toeplitz(x_taps, place), toeplitz(x_taps[::-1], place))
    lines = depth * rows
    lines_at = min(TILE, lines)
    top = chunk * rows

    def filter_x(band, store):
        wrap()
        for x in range(0, width, TILE):
            source = (lax.broadcasted_iota(jnp.int32, (window, 1), 0) + (x - LANES + width)) % width
            target = lax.broadcasted_iota(jnp.int32, (1, TILE), 1) + x
            apart = x_position(source, width, shift, flip_x) - x_position(target, width, shift, flip_x)
            cut = split(jnp.where(jnp.abs(apart) <= radius, band, 0.0))
            for line in range(0, lines, lines_at):
                at = slice(line, line + lines_at)
                cells = (high_ref[at, x : x + window], low_ref[at, x : x + window])
                store(line, x, dot3(cells, cut))

    blurred = {}

    def keep(line, x, value):
        blurred[line, x] = value

    filter_x(bands[0], keep)
    for (line, x), value in blurred.items():
        seen = meas_ref[line // rows : (line + lines_at) // rows, top : top + rows, x : x + TILE]
        high, low = split(seen.reshape(lines_at, TILE) / value)
        high_ref[line : line + lines_at, x + LANES : x + LANES + TILE] = high
        low_ref[line : line + lines_at, x + LANES : x + LANES + TILE] = low

    def keep_spread(line, x, value):
        work_ref[line // rows : (line + lines_at) // rows, :, x : x + TILE] = value.reshape(
            lines_at // rows, rows, TILE
        )

    filter_x(bands[1], keep_spread)

    @pl.loop(0, width // LANES)
    def _(index):
        lanes = pl.ds(pl.multiple_of(index * LANES, LANES), LANES)

        def store(z, value):
            out_ref[z, :, lanes] = value

        filter_z(lambda z: work_ref[z, :, lanes], store, z_taps[::-1])

    for index in range(depth):
        message, at = place_of(index, BACK, chunk, depth)
        leaving[message][at] = out_ref[me ^ index]


def product_kernel(psf_ref, factor_ref, *refs):
    me = lax.axis_index("slab")
    out_ref, work_ref = refs[-2:]
    chunks, slabs, step, width = work_ref.shape
    rows = step * chunks
    height = slabs * rows
    for chunk in range(chunks):
        for index in range(slabs):
            at, message = place_of(index, BACK, chunk, slabs)
            work_ref[chunk, me ^ index] = refs[first_message(BACK, chunk, slabs, -1) + message][at]
    taps = taps_of(psf_ref, 1)[::-1]
    lines = min(TILE, height)

    def block(first):
        start, window = y_window(first, height)
        targets = first + iota((lines, 1), 0)
        sources = y_cells(iota((1, window), 1), start, rows, chunks)
        band = y_band(taps, targets, sources)
        place, where = pl.ds(first, lines), pl.ds(start // rows, window // rows)
        for x in range(0, width, TILE):
            at = slice(x, x + TILE)
            cells = jnp.concatenate(
                [
                    work_ref[chunk, where, :, at].reshape(window // chunks, TILE)
                    for chunk in range(chunks)
                ]
            )
            out_ref[0, place, at] = factor_ref[0, place, at] * dot3(band, split(cells))

    if height == lines:
        block(0)
    else:
        pl.loop(0, height // lines)(lambda index: block(pl.multiple_of(index * lines, lines)))


SCALARS = pl.BlockSpec(memory_space=pltpu.SMEM)
WHOLE = pl.BlockSpec(memory_space=pltpu.VMEM)
PARAMS = pltpu.CompilerParams(vmem_limit_bytes=VMEM_BYTES)


def cost(moved):
    return pl.CostEstimate(flops=0, bytes_accessed=moved, transcendentals=0)


def body(estimate, measured, offsets, mirrors, psf):
    views = lax.axis_size("view")
    slabs = lax.axis_size("slab")
    _, height, width = estimate.shape
    _, depth, rows, _ = measured.shape
    step = rows // CHUNKS
    swap = [(i, (i + 1) % views) for i in range(views)]

    def shapes(plan, chunk):
        (first, _), (second, _) = order_of(plan, chunk, slabs)
        return [jax.ShapeDtypeStruct((second, step, width), jnp.float32)] * first

    def send(parts, unit):
        return [
            lax.ppermute(part, "slab", [(i, i ^ (k * unit)) for i in range(slabs)]) if k else part
            for k, part in enumerate(parts)
        ]

    def exchange(parts, plan, chunk):
        (_, first_unit), (second, second_unit) = order_of(plan, chunk, slabs)
        parts = send(parts, first_unit)
        return send([jnp.stack([part[at] for part in parts]) for at in range(second)], second_unit)

    sent = [None] * CHUNKS
    for chunk in reversed(range(CHUNKS)):
        order = [] if chunk == CHUNKS - 1 else sent[chunk + 1][:1]
        sent[chunk] = pl.pallas_call(
            functools.partial(blur_y_kernel, chunk),
            out_shape=shapes(THERE, chunk),
            in_specs=[SCALARS, WHOLE] + [pl.BlockSpec(memory_space=pl.ANY)] * len(order),
            out_specs=[WHOLE] * len(shapes(THERE, chunk)),
            compiler_params=PARAMS,
            cost_estimate=cost(OTHER_BYTES),
            name="blur_y",
        )(psf, estimate, *order)
    moved = [exchange(parts, THERE, chunk) for chunk, parts in enumerate(sent)]

    seen = jnp.roll(measured[0], -offsets[0] * BLOCK, axis=2)
    seen = lax.cond(mirrors[0, 1] == 1, lambda arr: jnp.flip(arr, 2), lambda arr: arr, seen)
    seen = lax.cond(mirrors[0, 0] == 1, lambda arr: jnp.flip(arr, 0), lambda arr: arr, seen)

    spread = [None] * CHUNKS
    for chunk in reversed(range(CHUNKS)):
        spread[chunk] = pl.pallas_call(
            functools.partial(ratio_kernel, chunk),
            out_shape=shapes(BACK, chunk),
            in_specs=[SCALARS, SCALARS, SCALARS] + [WHOLE] * (1 + len(moved[chunk])),
            out_specs=[WHOLE] * len(shapes(BACK, chunk)),
            scratch_shapes=[
                pltpu.VMEM((depth, step, width), jnp.float32),
                pltpu.VMEM((depth, step, width), jnp.float32),
                pltpu.VMEM((depth * step, width + 2 * LANES), jnp.bfloat16),
                pltpu.VMEM((depth * step, width + 2 * LANES), jnp.bfloat16),
            ],
            compiler_params=PARAMS,
            cost_estimate=cost(RATIO_BYTES),
            name="ratio",
        )(offsets, mirrors, psf, seen, *moved[chunk])
        seen, _ = lax.optimization_barrier((seen, spread[chunk][0]))
    own, other = [], []
    for chunk in range(CHUNKS):
        returned = exchange(spread[chunk], BACK, chunk)
        own += returned
        if BACK[chunk] == "hl":
            swapped = lax.ppermute(jnp.concatenate(returned[1:]), "view", swap)
            other.append(lax.ppermute(returned[0], "view", swap))
            other += jnp.split(swapped, len(returned) - 1)
        else:
            other += [lax.ppermute(part, "view", swap) for part in returned]
    late_psf, _ = lax.optimization_barrier((psf, own[0]))
    other_psf = lax.ppermute(late_psf, "view", swap)

    def multiply(psf, factor, messages):
        return pl.pallas_call(
            product_kernel,
            out_shape=jax.ShapeDtypeStruct(estimate.shape, jnp.float32),
            in_specs=[SCALARS] + [WHOLE] * (1 + len(messages)),
            out_specs=WHOLE,
            scratch_shapes=[pltpu.VMEM((CHUNKS, slabs, step, width), jnp.float32)],
            compiler_params=PARAMS,
            cost_estimate=cost(OTHER_BYTES),
            name="product",
        )(psf, factor, *messages)

    return multiply(other_psf, multiply(psf, estimate, own), other)


def solution(mesh):
    placed = (
        P("slab", None, None),
        P("view", None, "slab", None),
        P("view"),
        P("view", None),
        P("view", None, None),
    )
    return jax.shard_map(
        body, mesh=mesh, in_specs=placed, out_specs=P("slab", None, None), check_vma=False
    )
```

```python
import functools

import jax
import jax.numpy as jnp
from jax import lax
from jax.experimental import pallas as pl
from jax.experimental.pallas import tpu as pltpu
from jax.sharding import PartitionSpec as P

BLOCK = 64
TILE = 256
LANES = 128
CHUNKS = 2
LOW = 4
PACKED = 16
RATIO_BYTES = 12 * 1024 * 1024
OTHER_BYTES = 6 * 1024 * 1024
VMEM_BYTES = 48 * 1024 * 1024


def split(value):
    high = value.astype(jnp.bfloat16)
    low = (value - high.astype(jnp.float32)).astype(jnp.bfloat16)
    return high, low


def dot3(left, right):
    def dot(a, b):
        return jnp.dot(a, b, preferred_element_type=jnp.float32)

    return dot(left[0], right[0]) + (dot(left[0], right[1]) + dot(left[1], right[0]))


def toeplitz(taps, place):
    out = jnp.zeros(place.shape, jnp.float32)
    for index, tap in enumerate(taps):
        out = jnp.where(place == index, tap, out)
    return out


def y_cells(index, start, rows, chunks):
    step = rows // chunks
    count = index.shape[0] * index.shape[1] // chunks
    chunk = index // count
    within = index % count
    return start + (within // step) * rows + chunk * step + within % step


def y_band(taps, targets, sources):
    return split(toeplitz(taps, sources - targets + len(taps) // 2))


def y_window(first, height):
    window = min(2 * TILE, height)
    if height <= TILE:
        return 0, window
    return pl.multiple_of(jnp.clip(first - LANES, 0, height - window), LANES), window


def taps_of(psf_ref, row):
    return [psf_ref[0, row, t] for t in range(psf_ref.shape[2])]


def iota(shape, dimension):
    return lax.broadcasted_iota(jnp.int32, shape, dimension)


THERE = ("lh", "hl")
BACK = ("lh", "hl")


def order_of(plan, chunk, slabs):
    digits = {"l": (LOW, 1), "h": (slabs // LOW, LOW)}
    return tuple(digits[name] for name in plan[chunk])


def place_of(index, plan, chunk, slabs):
    return tuple(index // unit % radix for radix, unit in order_of(plan, chunk, slabs))


def first_message(plan, chunk, slabs, stage):
    return sum(order_of(plan, c, slabs)[stage][0] for c in range(chunk))


def blur_y_kernel(chunk, psf_ref, est_ref, *refs):
    out_refs = refs[-LOW:] if THERE[chunk] == "lh" else refs
    me = lax.axis_index("slab")
    height, width = est_ref.shape[1:]
    step = out_refs[0].shape[1]
    rows = step * CHUNKS
    slabs = height // rows
    lines = min(TILE, height) // CHUNKS
    blocks = lines // step
    taps = taps_of(psf_ref, 1)
    line = iota((lines, 1), 0)
    for group in range(slabs // blocks):
        targets = ((line // step + group * blocks) ^ me) * rows + chunk * step + line % step
        first = ((group * blocks) ^ (me // blocks * blocks)) * rows
        start, window = y_window(first, height)
        band = y_band(taps, targets, start + iota((1, window), 1))
        for x in range(0, width, TILE):
            value = dot3(band, split(est_ref[0, pl.ds(start, window), x : x + TILE]))
            for block in range(blocks):
                message, at = place_of(group * blocks + block, THERE, chunk, slabs)
                out_refs[message][at, :, x : x + TILE] = value[block * step : (block + 1) * step]


def x_position(cell, width, shift, flip):
    place = jnp.where(flip, width - 1 - cell, cell) + shift
    return jnp.where(place >= width, place - width, place)


def ratio_kernel(chunk, offset_ref, mirror_ref, psf_ref, meas_ref, *refs):
    work_ref, out_ref, high_ref, low_ref = refs[-4:]
    me = lax.axis_index("slab")
    depth, rows, width = work_ref.shape
    last = order_of(THERE, chunk, depth)[-1][0]
    arrived, leaving = refs[:last], refs[last:-4]
    for index in range(depth):
        at, message = place_of(index, THERE, chunk, depth)
        work_ref[me ^ index] = arrived[message][at]
    tap_count = psf_ref.shape[2]
    radius = tap_count // 2
    flip_z = mirror_ref[0, 0] == 1
    flip_x = mirror_ref[0, 1] == 1
    shift = offset_ref[0] * BLOCK

    def oriented(row, flip):
        taps = taps_of(psf_ref, row)
        return [jnp.where(flip, taps[tap_count - 1 - t], taps[t]) for t in range(tap_count)]

    z_taps = oriented(0, flip_z)
    x_taps = oriented(2, flip_x)

    def filter_z(load, store, taps):
        for z in range(depth):
            total = None
            for t in range(tap_count):
                source = z + t - radius
                if 0 <= source < depth:
                    term = taps[t] * load(source)
                    total = term if total is None else total + term
            store(z, total)

    group = max(1, PACKED // rows)

    @pl.loop(0, width // LANES)
    def _(index):
        lanes = pl.ds(pl.multiple_of(index * LANES, LANES), LANES)
        inner = pl.ds(pl.multiple_of((index + 1) * LANES, LANES), LANES)
        held = []

        def put(z, value):
            held.append(value)
            if len(held) == group:
                high, low = split(jnp.concatenate(held))
                where = pl.ds((z + 1 - group) * rows, group * rows)
                high_ref[where, inner] = high
                low_ref[where, inner] = low
                held.clear()

        filter_z(lambda z: work_ref[z, :, lanes], put, z_taps)

    def wrap():
        for ref in (high_ref, low_ref):
            ref[:, 0:LANES] = ref[:, width : width + LANES]
            ref[:, width + LANES : width + 2 * LANES] = ref[:, LANES : 2 * LANES]

    window = TILE + 2 * LANES
    tall = LANES + 2 * PACKED
    place = iota((tall, LANES), 0) - iota((tall, LANES), 1) + (radius - PACKED)
    bands = (toeplitz(x_taps, place), toeplitz(x_taps[::-1], place))

    def cut_band(band, x):
        columns = []
        for column in range(0, TILE, LANES):
            above = column + LANES - PACKED
            source = (iota((tall, 1), 0) + (x + column - PACKED + width)) % width
            target = iota((1, LANES), 1) + (x + column)
            apart = x_position(source, width, shift, flip_x) - x_position(target, width, shift, flip_x)
            parts = split(jnp.where(jnp.abs(apart) <= radius, band, 0.0))
            columns.append(
                [
                    jnp.concatenate(
                        [
                            jnp.zeros((above, LANES), part.dtype),
                            part,
                            jnp.zeros((window - above - tall, LANES), part.dtype),
                        ]
                    )
                    for part in parts
                ]
            )
        return [jnp.concatenate(parts, axis=1) for parts in zip(*columns)]

    lines = depth * rows
    lines_at = min(TILE, lines)
    top = chunk * rows

    def filter_x(band, store):
        wrap()
        for x in range(0, width, TILE):
            cut = cut_band(band, x)
            for line in range(0, lines, lines_at):
                at = slice(line, line + lines_at)
                cells = (high_ref[at, x : x + window], low_ref[at, x : x + window])
                store(line, x, dot3(cells, cut))

    blurred = {}

    def keep(line, x, value):
        blurred[line, x] = value

    filter_x(bands[0], keep)
    for (line, x), value in blurred.items():
        seen = meas_ref[line // rows : (line + lines_at) // rows, top : top + rows, x : x + TILE]
        high, low = split(seen.reshape(lines_at, TILE) / value)
        high_ref[line : line + lines_at, x + LANES : x + LANES + TILE] = high
        low_ref[line : line + lines_at, x + LANES : x + LANES + TILE] = low

    def keep_spread(line, x, value):
        work_ref[line // rows : (line + lines_at) // rows, :, x : x + TILE] = value.reshape(
            lines_at // rows, rows, TILE
        )

    filter_x(bands[1], keep_spread)

    @pl.loop(0, width // LANES)
    def _(index):
        lanes = pl.ds(pl.multiple_of(index * LANES, LANES), LANES)

        def store(z, value):
            out_ref[z, :, lanes] = value

        filter_z(lambda z: work_ref[z, :, lanes], store, z_taps[::-1])

    for index in range(depth):
        message, at = place_of(index, BACK, chunk, depth)
        leaving[message][at] = out_ref[me ^ index]


def product_kernel(psf_ref, factor_ref, *refs):
    me = lax.axis_index("slab")
    out_ref, work_ref = refs[-2:]
    chunks, slabs, step, width = work_ref.shape
    rows = step * chunks
    height = slabs * rows
    for chunk in range(chunks):
        for index in range(slabs):
            at, message = place_of(index, BACK, chunk, slabs)
            work_ref[chunk, me ^ index] = refs[first_message(BACK, chunk, slabs, -1) + message][at]
    taps = taps_of(psf_ref, 1)[::-1]
    lines = min(TILE, height)

    def block(first):
        start, window = y_window(first, height)
        targets = first + iota((lines, 1), 0)
        sources = y_cells(iota((1, window), 1), start, rows, chunks)
        band = y_band(taps, targets, sources)
        place, where = pl.ds(first, lines), pl.ds(start // rows, window // rows)
        for x in range(0, width, TILE):
            at = slice(x, x + TILE)
            cells = jnp.concatenate(
                [
                    work_ref[chunk, where, :, at].reshape(window // chunks, TILE)
                    for chunk in range(chunks)
                ]
            )
            out_ref[0, place, at] = factor_ref[0, place, at] * dot3(band, split(cells))

    if height == lines:
        block(0)
    else:
        pl.loop(0, height // lines)(lambda index: block(pl.multiple_of(index * lines, lines)))


SCALARS = pl.BlockSpec(memory_space=pltpu.SMEM)
WHOLE = pl.BlockSpec(memory_space=pltpu.VMEM)
PARAMS = pltpu.CompilerParams(vmem_limit_bytes=VMEM_BYTES)


def cost(moved):
    return pl.CostEstimate(flops=0, bytes_accessed=moved, transcendentals=0)


def body(estimate, measured, offsets, mirrors, psf):
    views = lax.axis_size("view")
    slabs = lax.axis_size("slab")
    _, height, width = estimate.shape
    _, depth, rows, _ = measured.shape
    step = rows // CHUNKS
    swap = [(i, (i + 1) % views) for i in range(views)]

    def shapes(plan, chunk):
        (first, _), (second, _) = order_of(plan, chunk, slabs)
        return [jax.ShapeDtypeStruct((second, step, width), jnp.float32)] * first

    def send(parts, unit):
        return [
            lax.ppermute(part, "slab", [(i, i ^ (k * unit)) for i in range(slabs)]) if k else part
            for k, part in enumerate(parts)
        ]

    def exchange(parts, plan, chunk):
        (_, first_unit), (second, second_unit) = order_of(plan, chunk, slabs)
        parts = send(parts, first_unit)
        return send([jnp.stack([part[at] for part in parts]) for at in range(second)], second_unit)

    sent = [None] * CHUNKS
    for chunk in reversed(range(CHUNKS)):
        order = [] if chunk == CHUNKS - 1 else sent[chunk + 1][:1]
        sent[chunk] = pl.pallas_call(
            functools.partial(blur_y_kernel, chunk),
            out_shape=shapes(THERE, chunk),
            in_specs=[SCALARS, WHOLE] + [pl.BlockSpec(memory_space=pl.ANY)] * len(order),
            out_specs=[WHOLE] * len(shapes(THERE, chunk)),
            compiler_params=PARAMS,
            cost_estimate=cost(OTHER_BYTES),
            name="blur_y",
        )(psf, estimate, *order)
    moved = [exchange(parts, THERE, chunk) for chunk, parts in enumerate(sent)]

    seen = jnp.roll(measured[0], -offsets[0] * BLOCK, axis=2)
    seen = lax.cond(mirrors[0, 1] == 1, lambda arr: jnp.flip(arr, 2), lambda arr: arr, seen)
    seen = lax.cond(mirrors[0, 0] == 1, lambda arr: jnp.flip(arr, 0), lambda arr: arr, seen)

    spread = [None] * CHUNKS
    for chunk in reversed(range(CHUNKS)):
        spread[chunk] = pl.pallas_call(
            functools.partial(ratio_kernel, chunk),
            out_shape=shapes(BACK, chunk),
            in_specs=[SCALARS, SCALARS, SCALARS] + [WHOLE] * (1 + len(moved[chunk])),
            out_specs=[WHOLE] * len(shapes(BACK, chunk)),
            scratch_shapes=[
                pltpu.VMEM((depth, step, width), jnp.float32),
                pltpu.VMEM((depth, step, width), jnp.float32),
                pltpu.VMEM((depth * step, width + 2 * LANES), jnp.bfloat16),
                pltpu.VMEM((depth * step, width + 2 * LANES), jnp.bfloat16),
            ],
            compiler_params=PARAMS,
            cost_estimate=cost(RATIO_BYTES),
            name="ratio",
        )(offsets, mirrors, psf, seen, *moved[chunk])
        seen, _ = lax.optimization_barrier((seen, spread[chunk][0]))
    own, other = [], []
    for chunk in range(CHUNKS):
        returned = exchange(spread[chunk], BACK, chunk)
        own += returned
        if BACK[chunk] == "hl":
            swapped = lax.ppermute(jnp.concatenate(returned[1:]), "view", swap)
            other.append(lax.ppermute(returned[0], "view", swap))
            other += jnp.split(swapped, len(returned) - 1)
        else:
            other += [lax.ppermute(part, "view", swap) for part in returned]
    late_psf, _ = lax.optimization_barrier((psf, own[0]))
    other_psf = lax.ppermute(late_psf, "view", swap)

    def multiply(psf, factor, messages):
        return pl.pallas_call(
            product_kernel,
            out_shape=jax.ShapeDtypeStruct(estimate.shape, jnp.float32),
            in_specs=[SCALARS] + [WHOLE] * (1 + len(messages)),
            out_specs=WHOLE,
            scratch_shapes=[pltpu.VMEM((CHUNKS, slabs, step, width), jnp.float32)],
            compiler_params=PARAMS,
            cost_estimate=cost(OTHER_BYTES),
            name="product",
        )(psf, factor, *messages)

    return multiply(other_psf, multiply(psf, estimate, own), other)


def solution(mesh):
    placed = (
        P("slab", None, None),
        P("view", None, "slab", None),
        P("view"),
        P("view", None),
        P("view", None, None),
    )
    return jax.shard_map(
        body, mesh=mesh, in_specs=placed, out_specs=P("slab", None, None), check_vma=False
    )
```
